32 devices in a mesh: tm: 16 (over z, y, x), rhs: 2 (over core).
Axes of the slice: x: 2, y: 2, z: 4, core: 2. Of those that a mesh axis runs over, the one named last changes fastest.
Arguments:
- diag_blocks: float32 [64, 384, 384], P('tm')
- couplings: float32 [64, 384, 384], P('tm'), as said below
- arrow_coupling: float32 [64, 256, 384], P('tm', 'rhs')
- right_sides: float32 [64, 384, 128], P('tm', None, 'rhs')
- arrow_block: float32 [256, 256], P('rhs'), may hold values from -6 to 6
- arrow_rhs: float32 [256, 128], P(None, 'rhs'), may hold values from -6 to 6
Outputs:
- block_results: float32 [64, 384, 384], P('tm')
- coupling_results: float32 [64, 384, 384], P('tm')
- arrow_results: float32 [64, 256, 384], P('tm', 'rhs')
- rhs_results: float32 [64, 384, 128], P('tm', None, 'rhs')
- reduced_arrow: float32 [256, 256], P('rhs')
- reduced_arrow_rhs: float32 [256, 128], P(None, 'rhs')
The draws below stay inside these ranges and needn't reach their ends.
Inputs may be any that keep to these rules, and one draw needn't show every extreme that they name: couplings[0] is zero.
All inputs are finite; a program needn't handle non-finite values. Where the reference program divides by a largest or mean magnitude, that divisor is 1e-20 or more.
Results may differ from the reference program's by a relative error of at most 0.0001.
Values sent between devices are 32-bit elements; how exact they have to be, the bound alone decides.
A program may use at most 64 MiB of HBM per device.

```python
import jax
import jax.numpy as jnp
from jax import lax

B = 384
A = 256
R = 128
ITERS = 12
LEVELS = 2
T_SIZE = 64


def scale_roots(key):
    logs = jax.random.uniform(jax.random.fold_in(key, 101), (T_SIZE, B), jnp.float32, jnp.log(0.05), jnp.log(20.0))
    return jnp.sqrt(jnp.exp(logs))


def draw_diag_blocks(key, part):
    roots = scale_roots(key)
    noise = jax.random.uniform(jax.random.fold_in(key, 11), (T_SIZE, B, B), jnp.float32, -1.0, 1.0)
    inner = (noise + 0.6 * jnp.swapaxes(noise, 1, 2)) * (0.8 / B ** 0.5) + 2.5 * jnp.eye(B, dtype=jnp.float32)[None]
    return inner * roots[:, :, None] * roots[:, None, :]


def draw_couplings(key, part):
    roots = scale_roots(key)
    earlier = jnp.concatenate([roots[:1], roots[:-1]], axis=0)
    inner = jax.random.uniform(jax.random.fold_in(key, 22), (T_SIZE, B, B), jnp.float32, -1.0, 1.0) * (0.45 / B ** 0.5)
    keep_mask = (jnp.arange(T_SIZE) > 0).astype(jnp.float32)
    return inner * roots[:, :, None] * earlier[:, None, :] * keep_mask[:, None, None]


def draw_arrow_coupling(key, part):
    roots = scale_roots(key)
    ramp = jnp.sqrt(1.0 + 2.0 * jnp.arange(T_SIZE).astype(jnp.float32) / (T_SIZE - 1))
    spread = ramp * jnp.sqrt(6.0 / (B * T_SIZE))
    noise = jax.random.uniform(jax.random.fold_in(key, 31), (T_SIZE, A, B), jnp.float32, -1.0, 1.0)
    return noise * spread[:, None, None] * roots[:, None, :]


def draw_right_sides(key, part):
    roots = scale_roots(key)
    noise = jax.random.normal(jax.random.fold_in(key, 41), (T_SIZE, B, R), jnp.float32)
    return noise * roots[:, :, None]


def levels(key, extent, cuts, low, high):
    loudness, own = 1.0, jax.random.fold_in(key, 6)
    for position, shards_of in cuts:
        steps = jnp.exp(jax.random.uniform(jax.random.fold_in(own, position), (shards_of,), jnp.float32, low / len(cuts), high / len(cuts)))
        loudness = loudness * jnp.repeat(steps, extent[position] // shards_of).reshape([-1 if axis == position else 1 for axis in range(len(extent))])
    return loudness


def scatter_about(own_key, dims, scale, bound, split=(), held_as=jnp.bfloat16):
    array = jax.random.normal(own_key, dims, jnp.float32) * scale
    if len(split) > 0:
        array = levels(own_key, dims, split, -0.22, 0.18) * array
    return jnp.clip(array, min=-bound, max=bound).astype(held_as)


def setup_inputs(seed: int = 0) -> dict:
    splits = jax.random.split(jax.random.key(seed), 7)
    return {
        "diag_blocks": draw_diag_blocks(jax.random.fold_in(splits[6], 71), 0),
        "couplings": draw_couplings(jax.random.fold_in(splits[6], 71), 0),
        "arrow_coupling": draw_arrow_coupling(jax.random.fold_in(splits[6], 71), 0),
        "right_sides": draw_right_sides(jax.random.fold_in(splits[6], 71), 0),
        "arrow_block": scatter_about(splits[4], (A, A), 1.0, 6.0, ((0, 2),), jnp.float32),
        "arrow_rhs": scatter_about(splits[5], (A, R), 1.0, 6.0, ((1, 2),), jnp.float32),
    }


def product(left, right):
    return jnp.matmul(left, right, precision=lax.Precision.HIGHEST)


def flipped(matrix):
    return jnp.swapaxes(matrix, -1, -2)


def newton_inverse(blocks):
    identity = jnp.eye(blocks.shape[-1], dtype=blocks.dtype)
    row_bound = jnp.max(jnp.sum(jnp.abs(blocks), axis=-1), axis=-1)
    start_guess = identity[None] / row_bound[:, None, None]

    def sweep(counter, approx):
        return 2.0 * approx - product(approx, product(blocks, approx))

    return lax.fori_loop(0, ITERS, sweep, start_guess)


def shifted_down(values):
    return jnp.concatenate([jnp.zeros_like(values[:1]), values[:-1]], axis=0)


def reduce_level(diagonal, coupling, arrow, right):
    inverse = newton_inverse(diagonal[1::2])
    own_coupling = coupling[1::2]
    next_coupling = jnp.concatenate([coupling[2::2], jnp.zeros_like(coupling[:1])], axis=0)
    multiplier = product(inverse, own_coupling)
    solved = product(inverse, right[1::2])
    weighted = product(arrow[1::2], inverse)
    left_diag = product(flipped(own_coupling), multiplier)
    left_right = product(flipped(own_coupling), solved)
    left_arrow = product(weighted, own_coupling)
    next_diag = product(product(next_coupling, inverse), flipped(next_coupling))
    next_link = -product(next_coupling, multiplier)
    next_arrow = product(weighted, flipped(next_coupling))
    next_right = product(next_coupling, solved)
    kept_state = (diagonal[0::2] - shifted_down(next_diag) - left_diag,
                  shifted_down(next_link),
                  arrow[0::2] - shifted_down(next_arrow) - left_arrow,
                  right[0::2] - shifted_down(next_right) - left_right)
    gone = (inverse, multiplier, weighted, solved)
    block_term = jnp.sum(product(weighted, flipped(arrow[1::2])), axis=0)
    right_term = jnp.sum(product(weighted, right[1::2]), axis=0)
    return kept_state, gone, block_term, right_term


def reference(diag_blocks, couplings, arrow_coupling, right_sides, arrow_block, arrow_rhs):
    state = (diag_blocks, couplings, arrow_coupling, right_sides)
    results = [jnp.zeros_like(whole) for whole in state]
    block_total = jnp.zeros_like(arrow_block)
    right_total = jnp.zeros_like(arrow_rhs)
    for level_no in range(LEVELS):
        stride = 2 ** level_no
        state, gone, block_term, right_term = reduce_level(state[0], state[1], state[2], state[3])
        results = [whole.at[stride::2 * stride].set(piece) for whole, piece in zip(results, gone)]
        block_total = block_total + block_term
        right_total = right_total + right_term
    final_stride = 2 ** LEVELS
    results = [whole.at[0::final_stride].set(piece) for whole, piece in zip(results, state)]
    return (results[0], results[1], results[2], results[3], arrow_block - block_total, arrow_rhs - right_total)
```

```python
import functools

import jax
import jax.numpy as jnp
from jax import lax
from jax.experimental import pallas as pl
from jax.experimental.pallas import tpu as pltpu
from jax.sharding import PartitionSpec as P

ITERS = 12
F32, BF16 = jnp.float32, jnp.bfloat16
VMEM_BYTES = 48 * 2**20


def halves(value):
    high = value.astype(BF16)
    return high, (value - high.astype(F32)).astype(BF16)


def product(left, right):
    left_high, left_low = halves(left)
    right_high, right_low = halves(right)
    return lax.dot_general(
        jnp.concatenate([left_high, left_low, left_high], axis=1),
        jnp.concatenate([right_high, right_high, right_low], axis=0),
        (((1,), (0,)), ((), ())),
        preferred_element_type=F32,
    )


def beside(*parts):
    return jnp.concatenate(parts, axis=1)


def newton_inverse(block, both):
    n = block.shape[0]
    row_bound = jnp.max(jnp.sum(jnp.abs(block), axis=1, keepdims=True), axis=0, keepdims=True)
    scaled = block / row_bound
    rows = lax.broadcasted_iota(jnp.int32, (n, n), 0)
    identity = (rows == lax.broadcasted_iota(jnp.int32, (n, n), 1)).astype(F32)
    both[:, :n] = 2.0 * scaled - product(scaled, scaled)
    both[:, n:] = 2.0 * identity - scaled

    def sweep(_, carry):
        now = both[...]
        both[...] = 2.0 * now - product(now[:, :n], now)
        return carry

    lax.fori_loop(0, ITERS - 3, sweep, 0)
    approx = both[:, n:]
    approx = 2.0 * approx - product(both[:, :n], approx)
    approx = 2.0 * approx - product(product(approx, scaled), approx)
    return approx / row_bound


def either(core, first, second):
    return jnp.where(core == 0, first, second)


def joined(core, mine, other):
    return jnp.concatenate([either(core, mine, other), either(core, other, mine)], axis=0)


def first_inverse_kernel(core_ref, diag_ref, link_ref, inverse_ref, part_ref, both):
    core = core_ref[0]
    inverse = newton_inverse(diag_ref[0], both)
    inverse_ref[...] = inverse
    link = link_ref[0]
    factor = either(core, link, link.T)
    part_ref[...] = product(product(factor, inverse), factor.T)


def arrow_terms(core, weighted, arrow, arrow_other, solved):
    mine, other = product(weighted, arrow.T), product(weighted, arrow_other.T)
    block = beside(either(core, mine, other), either(core, other, mine))
    right = product(joined(core, arrow, arrow_other), solved)
    return block, right


def level_kernel(
    core_ref, mine_ref, other_ref, part_ref, part_other_ref, diag_ref, link_ref, arrow_ref,
    arrow_other_ref, right_ref,
    inverses_ref, multipliers_ref, weights_ref, solves_ref,
    diag2_ref, link2_ref, half2_ref, arrow2_ref, right2_ref, diag0_ref, arrow0_ref, right0_ref,
    block_ref, sum_ref,
):
    core = core_ref[0]
    n = mine_ref.shape[0]
    mine, other = mine_ref[...], other_ref[...]
    inverse1, inverse3 = either(core, mine, other), either(core, other, mine)
    inverses_ref[0, 0] = inverse1
    inverses_ref[1, 0] = inverse3
    diag2_ref[...] = diag_ref[2] - (part_ref[...] + part_other_ref[...])
    link1, link2, link3 = link_ref[1], link_ref[2], link_ref[3]
    solve1 = product(inverse1, beside(link1, right_ref[1]))
    multipliers_ref[0, 0] = solve1[:, :n]
    solves_ref[0, 0] = solve1[:, n:]
    after1 = product(jnp.concatenate([link2, link1.T], axis=0), solve1)
    new_link = -after1[:n, :n]
    link2_ref[...] = new_link
    m = n // 2
    half2_ref[...] = either(core, new_link[:m], new_link[m:])
    diag0_ref[...] = diag_ref[0] - after1[n:, :n]
    right0_ref[...] = right_ref[0] - after1[n:, n:]
    weighted1 = product(arrow_ref[1], inverse1)
    weights_ref[0, 0] = weighted1
    arrow_after1 = product(weighted1, beside(link2.T, link1))
    arrow0_ref[...] = arrow_ref[0] - arrow_after1[:, n:]
    solve3 = product(inverse3, beside(link3, right_ref[3]))
    multipliers_ref[1, 0] = solve3[:, :n]
    solves_ref[1, 0] = solve3[:, n:]
    right2_ref[...] = right_ref[2] - after1[:n, n:] - product(link3.T, solve3[:, n:])
    weighted3 = product(arrow_ref[3], inverse3)
    weights_ref[1, 0] = weighted3
    arrow2_ref[...] = arrow_ref[2] - arrow_after1[:, :n] - product(weighted3, link3)
    block1, sum1 = arrow_terms(core, weighted1, arrow_ref[1], arrow_other_ref[0], solve1[:, n:])
    block3, sum3 = arrow_terms(core, weighted3, arrow_ref[3], arrow_other_ref[1], solve3[:, n:])
    block_ref[...] = block1 + block3
    sum_ref[...] = sum1 + sum3


def second_inverse_kernel(core_ref, diag_ref, kept_ref, inverse_ref, half_ref, both):
    inverse = newton_inverse(diag_ref[...], both)
    inverse_ref[0, 0] = inverse
    m = inverse.shape[0] // 2
    half_ref[...] = either(core_ref[0], inverse[:m], inverse[m:])


def own_kernel(
    core_ref, inverse_ref, link_ref, arrow_ref, arrow_other_ref, right_ref, diag0_ref, arrow0_ref,
    right0_ref, block_ref, sum_ref, kept1, kept2, kept3,
    multiplier_out, weighted_out, solved_out, diag0_out, arrow0_out, right0_out, block_out, sum_out,
):
    core = core_ref[0]
    inverse, link, arrow = inverse_ref[0, 0], link_ref[...], arrow_ref[...]
    n = inverse.shape[0]
    weighted = product(arrow, inverse)
    weighted_out[0, 0] = weighted
    solve = product(inverse, beside(link, right_ref[...]))
    multiplier_out[0, 0] = solve[:, :n]
    solved_out[0, 0] = solve[:, n:]
    block, right = arrow_terms(core, weighted, arrow, arrow_other_ref[...], solve[:, n:])
    block_out[...] = block_ref[...] + block
    sum_out[...] = sum_ref[...] + right
    after = product(link.T, solve)
    diag0_out[...] = diag0_ref[...] - after[:, :n]
    right0_out[...] = right0_ref[...] - after[:, n:]
    arrow0_out[...] = arrow0_ref[...] - product(weighted, link)


def far_terms(core_ref, here_ref, x_ref, x_other_ref, l_ref, l_other_ref, arrow_ref, right_ref):
    core = core_ref[0]
    here = here_ref[...]
    n = here.shape[-1]
    here = here.reshape(n, n)
    inverse = joined(core, x_ref[...], x_other_ref[...])
    link = joined(core, l_ref[...], l_other_ref[...])
    flipped = here.T
    ahead = product(here, inverse)
    after = product(ahead, beside(flipped, link, right_ref[...]))
    arrow = product(product(arrow_ref[...], inverse), flipped)
    return after[:, :n], -after[:, n : 2 * n], arrow, after[:, 2 * n :]


def far_kernel(
    core_ref, here_ref, x_ref, x_other_ref, l_ref, l_other_ref, a_ref, r_ref,
    diag0_ref, arrow0_ref, right0_ref, diag0_out, link0_out, arrow0_out, right0_out,
):
    diag, link, arrow, right = far_terms(
        core_ref, here_ref, x_ref, x_other_ref, l_ref, l_other_ref, a_ref, r_ref
    )
    diag0_out[...] = diag0_ref[...] - diag
    link0_out[...] = link
    arrow0_out[...] = arrow0_ref[...] - arrow
    right0_out[...] = right0_ref[...] - right


def last_kernel(
    core_ref, here_ref, x_ref, x_other_ref, l_ref, l_other_ref, a_ref, r_ref,
    diag0_ref, arrow0_ref, right0_ref, kept1, kept2, kept3, kept4,
    diag0_out, link0_out, arrow0_out, right0_out,
):
    diag, link, arrow, right = far_terms(
        core_ref, here_ref, x_ref, x_other_ref, l_ref, l_other_ref, a_ref, r_ref
    )
    diag0_out[0, 0] = diag0_ref[...] - diag
    link0_out[0, 0] = link
    arrow0_out[0, 0] = arrow0_ref[...] - arrow
    right0_out[0, 0] = right0_ref[...] - right


def whole(array):
    zeros = (0,) * array.ndim
    return pl.BlockSpec(array.shape, lambda i, c: zeros)


def stored(shape, index=None, block=None):
    index = index or (0,) * len(shape)
    return jax.ShapeDtypeStruct(shape, F32), pl.BlockSpec(block or shape, lambda i, c: index)


def placed(shape, row, column):
    return stored((2, 2, *shape), (row, column, 0, 0), (1, 1, *shape))


KEPT = pl.BlockSpec(memory_space=pl.ANY)


def call(kernel, core, operands, outs, micros, scratch=(), aliases=None, name=None):
    specs = [spec or whole(array) for array, spec in operands]
    arrays = [array for array, spec in operands]
    return pl.pallas_call(
        kernel,
        out_shape=[shape for shape, spec in outs],
        grid_spec=pltpu.PrefetchScalarGridSpec(
            num_scalar_prefetch=1,
            grid=(1,),
            in_specs=specs,
            out_specs=[spec for shape, spec in outs],
            scratch_shapes=scratch,
        ),
        input_output_aliases=aliases or {},
        compiler_params=pltpu.CompilerParams(vmem_limit_bytes=VMEM_BYTES),
        cost_estimate=pl.CostEstimate(
            flops=int(micros * 1.15e9), bytes_accessed=2**20, transcendentals=0
        ),
        name=name,
    )(core, *arrays)


def per_device(diag_blocks, couplings, arrow_coupling, right_sides, arrow_block, arrow_rhs):
    count, n, _ = diag_blocks.shape
    a, r = arrow_coupling.shape[1], right_sides.shape[2]
    m = n // 2
    core_index = lax.axis_index("rhs")
    core = core_index.astype(jnp.int32).reshape(1)
    length = lax.axis_size("tm")
    route = [(i, i + 1) for i in range(length - 1)]

    def to_next(value):
        return lax.ppermute(value, "tm", route)

    def swapped(value):
        return lax.ppermute(value, "rhs", [(0, 1), (1, 0)])

    def half_of(value):
        return lax.dynamic_slice_in_dim(value, core_index * m, m, 0)

    link3_half = to_next(lax.dynamic_slice(couplings, (3, core_index * m, 0), (1, m, n))[0])
    arrow3_far = to_next(arrow_coupling[3])
    right3_far = to_next(right_sides[3])
    arrow_other = swapped(jnp.stack([arrow_coupling[1], arrow_coupling[3]]))

    both = [pltpu.VMEM((n, 2 * n), F32)]
    one = (1, n, n)
    mine, part = call(
        first_inverse_kernel,
        core,
        [
            (diag_blocks, pl.BlockSpec(one, lambda i, c: (1 + 2 * c[0], 0, 0))),
            (couplings, pl.BlockSpec(one, lambda i, c: (2 + c[0], 0, 0))),
        ],
        [stored((n, n)), stored((n, n))],
        15,
        both,
        name="first_inverse",
    )
    part_other, other = swapped(part), swapped(mine)
    inverse3_half = to_next(half_of(jnp.where(core_index == 0, other, mine)))

    def odd(shape):
        return stored((2, 2, *shape), (0, 1, 0, 0), (2, 1, *shape))

    (
        inverses, multipliers, weights, solves, diag2, link2, link2_mine, arrow2, right2, diag0,
        arrow0, right0, block_sum, right_sum,
    ) = call(
        level_kernel,
        core,
        [
            (x, None)
            for x in (
                mine, other, part, part_other, diag_blocks, couplings, arrow_coupling,
                arrow_other, right_sides,
            )
        ],
        [odd((n, n)), odd((n, n)), odd((a, n)), odd((n, r))]
        + [stored(s) for s in ((n, n), (n, n), (m, n), (a, n), (n, r), (n, n), (a, n), (n, r))]
        + [stored(arrow_block.shape), stored(arrow_rhs.shape)],
        8,
        name="level",
    )
    link2_half = to_next(link2_mine)
    arrow2_far = to_next(arrow2)
    right2_far = to_next(right2)
    link3_other = swapped(link3_half)
    arrow2_other = swapped(arrow2)

    inverses, inverse2_mine = call(
        second_inverse_kernel,
        core,
        [(diag2, None), (inverses, KEPT)],
        [placed((n, n), 1, 0), stored((m, n))],
        13,
        both,
        {2: 0},
        name="second_inverse",
    )
    inverse2_half = to_next(inverse2_mine)
    inverse3_other = swapped(inverse3_half)
    link2_other = swapped(link2_half)

    two = pl.BlockSpec((1, 1, n, n), lambda i, c: (1, 0, 0, 0))
    multipliers, weights, solves, diag0, arrow0, right0, block_sum, right_sum = call(
        own_kernel,
        core,
        [(inverses, two)]
        + [
            (x, None)
            for x in (
                link2, arrow2, arrow2_other, right2, diag0, arrow0, right0, block_sum, right_sum
            )
        ]
        + [(multipliers, KEPT), (weights, KEPT), (solves, KEPT)],
        [placed((n, n), 1, 0), placed((a, n), 1, 0), placed((n, r), 1, 0)]
        + [stored(x.shape) for x in (diag0, arrow0, right0, block_sum, right_sum)],
        3,
        aliases={11: 0, 12: 1, 13: 2},
        name="own",
    )
    block_total, right_total = lax.psum((block_sum, right_sum), "tm")

    first_link = (couplings, pl.BlockSpec(one, lambda i, c: (0, 0, 0)))
    diag0, link0, arrow0, right0 = call(
        far_kernel,
        core,
        [first_link]
        + [
            (x, None)
            for x in (
                inverse3_half, inverse3_other, link3_half, link3_other, arrow3_far, right3_far,
                diag0, arrow0, right0,
            )
        ],
        [stored((n, n)), stored((n, n)), stored((a, n)), stored((n, r))],
        3,
        name="far",
    )
    inverse2_other = swapped(inverse2_half)
    inverses, multipliers, weights, solves = call(
        last_kernel,
        core,
        [
            (x, None)
            for x in (
                link0, inverse2_half, inverse2_other, link2_half, link2_other, arrow2_far,
                right2_far, diag0, arrow0, right0,
            )
        ]
        + [(x, KEPT) for x in (inverses, multipliers, weights, solves)],
        [placed((n, n), 0, 0), placed((n, n), 0, 0), placed((a, n), 0, 0), placed((n, r), 0, 0)],
        3,
        aliases={11: 0, 12: 1, 13: 2, 14: 3},
        name="last",
    )
    return (
        inverses.reshape(diag_blocks.shape),
        multipliers.reshape(couplings.shape),
        weights.reshape(arrow_coupling.shape),
        solves.reshape(right_sides.shape),
        arrow_block - block_total,
        arrow_rhs - right_total,
    )


def solution(mesh):
    return jax.shard_map(
        per_device,
        mesh=mesh,
        in_specs=(
            P("tm", None, None),
            P("tm", None, None),
            P("tm", "rhs", None),
            P("tm", None, "rhs"),
            P("rhs", None),
            P(None, "rhs"),
        ),
        out_specs=(
            P("tm", None, None),
            P("tm", None, None),
            P("tm", "rhs", None),
            P("tm", None, "rhs"),
            P("rhs", None),
            P(None, "rhs"),
        ),
        check_vma=False,
    )
```
